256 devices in a mesh: row: 32 (over z_hi, x, core), col: 8 (over y, z_lo).
Axes of the slice: x: 4, y: 4, z: 8 (z_hi: 4, z_lo: 2; z = z_hi * 2 + z_lo), core: 2. Of those that a mesh axis runs over, the one named last changes fastest.
Arguments:
- pair_valence: int32 [4096], P(('row', 'col')), may hold values from 0 to 63
- pair_conduction: int32 [4096], P(('row', 'col')), may hold values from 0 to 3071
- elements: bfloat16 [4096, 12288], P(('row', 'col')), may hold values from -0.09375 to 0.09375
- valence_energy: float32 [64], replicated, may hold values from -12 to -0.5
- conduction_energy: float32 [3072], replicated, may hold values from 0.5 to 25
- coulomb_sqrt: float32 [12288], replicated, may hold values from 0.3 to 3
Outputs:
- chi_sym: float32 [12288, 12288], P('row', 'col')
The draws below stay inside these ranges and needn't reach their ends.
All inputs are finite; a program needn't handle non-finite values.
Results may differ from the reference program's by a relative error of at most 0.0025.
Values may be sent and summed in bfloat16 or wider, within the bound.
A program may use at most 128 MiB of HBM per device.

```python
import math
import jax
import jax.numpy as jnp

NG = 12288
NV = 64
NC = 3072
PAIRS = 4096


def set_ends(result, rng, least, top_value):
    longest = result.shape.index(max(result.shape))
    spots = []
    for shift in (0, 1):
        where = [jax.random.randint(jax.random.fold_in(rng, axis), (), 0, length) for axis, length in enumerate(result.shape)]
        where[longest] = (where[longest] + shift) % result.shape[longest]
        spots.append(tuple(where))
    return result.at[spots[0]].set(least).at[spots[1]].set(top_value)


def block_scale(own_key, extent, split, low, high):
    def one(axis_at, shards_of):
        steps = jax.random.uniform(jax.random.fold_in(jax.random.fold_in(own_key, 6), axis_at), (shards_of,), jnp.float32, low / len(split), high / len(split))
        return jnp.repeat(jnp.exp(steps), extent[axis_at] // shards_of).reshape((-1,) + (1,) * (len(extent) - axis_at - 1))

    gain = one(*split[0])
    for cut in split[1:]:
        gain = gain * one(*cut)
    return gain


def scatter_about(rng, extent, spread, most, pieces=(), dtype=jnp.bfloat16):
    loudness = block_scale(rng, extent, pieces, -0.22, 0.18) if pieces else 1.0
    result = jax.random.normal(rng, extent, jnp.float32) * spread * loudness
    return jnp.minimum(jnp.maximum(result, -most), most).astype(dtype)


def setup_inputs(seed: int = 0) -> dict:
    streams_of = jax.random.split(jax.random.key(seed), 7)
    return {
        "pair_valence": set_ends(jax.random.randint(streams_of[0], (PAIRS,), 0, NV), jax.random.fold_in(streams_of[0], 1), 0, NV - 1).astype(jnp.int32),
        "pair_conduction": set_ends(jax.random.randint(streams_of[1], (PAIRS,), 0, NC), jax.random.fold_in(streams_of[1], 1), 0, NC - 1).astype(jnp.int32),
        "elements": scatter_about(streams_of[2], (PAIRS, NG), PAIRS ** -0.5, 0.09375, ((0, 256),)),
        "valence_energy": jnp.clip(jax.random.uniform(streams_of[3], (NV,), jnp.float32, -12.0, -0.5), -12.0, -0.5),
        "conduction_energy": jnp.clip(jax.random.uniform(streams_of[4], (NC,), jnp.float32, 0.5, 25.0), 0.5, 25.0),
        "coulomb_sqrt": jnp.clip(jnp.exp(jax.random.uniform(streams_of[5], (NG,), jnp.float32, math.log(0.3), math.log(3.0))), 0.3, 3.0),
    }


def reference(pair_valence, pair_conduction, elements, valence_energy, conduction_energy, coulomb_sqrt):
    lower = jnp.take(valence_energy, pair_valence, axis=0)
    upper = jnp.take(conduction_energy, pair_conduction, axis=0)
    weight = 4.0 / (lower - upper)
    scaled = (weight[:, None] * elements.astype(jnp.float32)).astype(jnp.bfloat16)
    chi_zero = jnp.dot(scaled.T, elements, preferred_element_type=jnp.float32)
    return coulomb_sqrt[:, None] * chi_zero * coulomb_sqrt[None, :]
```

```python
import functools

import jax
import jax.numpy as jnp
from jax import lax
from jax.experimental import pallas as pl
from jax.experimental.pallas import tpu as pltpu
from jax.sharding import PartitionSpec as P

MESH = pl.DeviceIdType.MESH
F32, BF16 = jnp.float32, jnp.bfloat16

PAIRS_HERE = 16
WIDE = 1536
HALF = WIDE // 2
QUARTER = WIDE // 4
CHUNKS = ((0, 256), (256, 256), (512, 256), (768, 256), (1024, 256), (1280, 256))
GROUPS = ((0, 512), (512, 512), (1024, 512))


def kernel(
    val_ref, cond_ref, e_ref, ve_ref, ce_ref, cs_ref, out_ref,
    es, a_in, at, bp, c_give, c_keep, c_got, p_give, p_got, out_v,
    a2a_s, a2a_r, ag_s, ag_r, bg_s, bg_r, c_s, c_r, p_s, p_r, o_s,
):
    row, col = lax.axis_index("row"), lax.axis_index("col")
    core, x, zh = row % 2, (row // 2) % 4, row // 8
    y, zl = col // 2, col % 2
    xh, xl = x // 2, x % 2

    def device(x_, y_, zh_, zl_, core_):
        return ((zh_ * 4 + x_) * 2 + core_, y_ * 2 + zl_)

    pair_peers = []
    for mirror in (0, 1):
        for dz in range(4):
            if mirror or dz:
                x_ = 3 - x if mirror else x
                pair_peers.append((x_, (zh + dz) % 4))
    block_peers = [((y + d // 2) % 4, (zl + d % 2) % 2) for d in range(1, 8)]
    other_core = device(x, y, zh, zl, 1 - core)
    neighbour = device(x + 1 - 2 * xl, y, zh, zl, core)
    mirror_dev = device(3 - x, y, zh, zl, core)
    z_up = device(x, y, (zh + 1) % 4, zl, core)
    z_down = device(x, y, (zh + 3) % 4, zl, core)
    z_mate = device(x, y, zh, 1 - zl, core)
    y_up = device(x, (y + 1) % 4, zh, zl, core)
    y_down = device(x, (y + 3) % 4, zh, zl, core)

    barrier = pltpu.get_barrier_semaphore()
    everyone = [device(x_, y, zh_, zl, core) for x_, zh_ in pair_peers]
    everyone += [device(x, y_, zh, zl_, core) for y_, zl_ in block_peers]
    everyone += [other_core, neighbour]
    for peer in everyone:
        pl.semaphore_signal(barrier, inc=1, device_id=peer, device_id_type=MESH)

    sent = []

    def send(src, dst, send_sem, recv_sem, peer):
        copy = pltpu.make_async_remote_copy(
            src_ref=src, dst_ref=dst, send_sem=send_sem, recv_sem=recv_sem,
            device_id=peer, device_id_type=MESH,
        )
        copy.start()
        return copy

    def pick(idx_ref, table):
        slots = lax.broadcasted_iota(jnp.int32, table.shape, 0) * table.shape[1]
        slots += lax.broadcasted_iota(jnp.int32, table.shape, 1)
        rows = [
            jnp.sum(jnp.where(slots == idx_ref[i], table, 0.0), axis=0, keepdims=True)
            for i in range(PAIRS_HERE)
        ]
        return jnp.sum(jnp.concatenate(rows, axis=0), axis=1, keepdims=True)

    weight = 4.0 / (pick(val_ref, ve_ref[...]) - pick(cond_ref, ce_ref[...]))
    for j in range(0, e_ref.shape[1], HALF):
        part = e_ref[:, j : j + HALF].astype(F32)
        es[:, j : j + HALF] = (weight * part).astype(BF16)

    pl.semaphore_wait(barrier, len(everyone))

    spot = xh * 4 + zh
    deep = pl.ds(spot * PAIRS_HERE, PAIRS_HERE)

    def send_b(g):
        start, width = GROUPS[g]
        copies = []
        for y_, zl_ in block_peers:
            c_ = y_ * 2 + zl_
            cols = pl.ds(pl.multiple_of(c_ * WIDE + start, 256), width)
            copies.append(
                send(
                    e_ref.at[:, cols],
                    bp.at[col, spot, :, pl.ds(start, width)],
                    a2a_s.at[2 + g], a2a_r.at[2 + g],
                    device(x, y_, zh, zl_, core),
                )
            )
        cols = pl.ds(pl.multiple_of(col * WIDE + start, 256), width)
        bp[col, spot, :, pl.ds(start, width)] = e_ref[:, cols]

    def wait_b(g):
        start, width = GROUPS[g]
        ref = bp.at[pl.ds(0, 7), 0, :, pl.ds(start, width)]
        pltpu.make_async_copy(ref, ref, a2a_r.at[2 + g]).wait()

    def send_a(h):
        def cols_of(x_, zh_):
            part = 1 - x_ % 2 if h == 0 else x_ % 2
            return pl.ds(pl.multiple_of((zh_ * 2 + x_ // 2) * WIDE + part * HALF, 256), HALF)

        for x_, zh_ in pair_peers:
            send(
                es.at[:, cols_of(x_, zh_)], a_in.at[h, deep, :],
                a2a_s.at[h], a2a_r.at[h], device(x_, y, zh_, zl, core),
            )
        a_in[h, deep, :] = es[:, cols_of(x, zh)]

    def wait_a(h):
        ref = a_in.at[h, pl.ds(0, 7 * PAIRS_HERE), :]
        pltpu.make_async_copy(ref, ref, a2a_r.at[h]).wait()

    mate = y * 2 + 1 - zl
    up2, down2 = (y + 1) % 4 * 2, (y + 3) % 4 * 2

    def ag(h, n, slot, peer, rows=None):
        ref = at.at[h, slot] if rows is None else at.at[h, slot, pl.ds(*rows)]
        copy = send(ref, ref, ag_s.at[h, n], ag_r.at[h, n], peer)
        sent.append(copy)
        return copy

    def a_first(h):
        wait_a(h)
        at[h, col] = a_in[h].T
        return [ag(h, 0, col, z_mate), ag(h, 1, col, y_up), ag(h, 2, col, y_down)]

    def a_second(h, first):
        first[0].wait_recv()
        return [ag(h, 3, mate, y_up), ag(h, 4, mate, y_down)]

    lo, hi = (0, QUARTER), (QUARTER, QUARTER)

    def a_third(h, first):
        first[1].wait_recv()
        one = ag(h, 5, down2 + zl, y_up, lo)
        first[2].wait_recv()
        return [one, ag(h, 6, up2 + zl, y_down, hi)]

    def a_fourth(h, second):
        second[0].wait_recv()
        one = ag(h, 7, down2 + 1 - zl, y_up, lo)
        second[1].wait_recv()
        return [one, ag(h, 8, up2 + 1 - zl, y_down, hi)]

    def a_last(copies):
        for copy in copies:
            copy.wait_recv()

    s_up, s_down, s_far = (xh * 4 + (zh + d) % 4 for d in (1, 3, 2))

    def bg(j, n, s, peer, rows=None):
        start, width = CHUNKS[j]
        rows = pl.ds(0, 8) if rows is None else pl.ds(*rows)
        ref = bp.at[rows, s, :, pl.ds(start, width)]
        copy = send(ref, ref, bg_s.at[j, n], bg_r.at[j, n], peer)
        sent.append(copy)
        return copy

    chunks = [dict() for _ in CHUNKS]

    def b_first(j):
        d = chunks[j]
        d["up"] = bg(j, 0, spot, z_up)
        d["down"] = bg(j, 1, spot, z_down)
        d["m0"] = bg(j, 2, spot, mirror_dev)

    def b_second(j):
        d = chunks[j]
        d["up"].wait_recv()
        d["far0"] = bg(j, 3, s_down, z_up, (0, 4))
        d["m1"] = bg(j, 4, s_down, mirror_dev)
        d["down"].wait_recv()
        d["far1"] = bg(j, 5, s_up, z_down, (4, 4))
        d["m2"] = bg(j, 6, s_up, mirror_dev)

    def b_third(j):
        d = chunks[j]
        d["far0"].wait_recv()
        d["far1"].wait_recv()
        d["m3"] = bg(j, 7, s_far, mirror_dev)

    def b_last(j):
        for n in range(4):
            chunks[j][f"m{n}"].wait_recv()

    def product(j, h, q):
        start, width = CHUNKS[j]
        rows = pl.ds(pl.multiple_of(q * QUARTER, QUARTER), QUARTER)
        left = jnp.concatenate([at[h, n, rows, :] for n in range(8)], axis=1)
        right = bp[:, :, :, start : start + width].reshape(1024, width)
        return jnp.dot(left, right, preferred_element_type=F32)

    def multiply(j, h):
        start, width = CHUNKS[j]
        cols = pl.ds(start, width)
        c_give[h, :, cols] = product(j, h, 1 - core)
        copy = send(
            c_give.at[h, :, cols], c_got.at[h, :, cols], c_s.at[j, h], c_r.at[j, h], other_core
        )
        sent.append(copy)
        chunks[j][f"c{h}"] = copy
        c_keep[h, :, cols] = product(j, h, core)

    def give(j):
        start, width = CHUNKS[j]
        cols = pl.ds(start, width)
        chunks[j]["c0"].wait_recv()
        p_give[:, cols] = (c_keep[0, :, cols] + c_got[0, :, cols]).astype(BF16)
        copy = send(p_give.at[:, cols], p_got.at[:, cols], p_s.at[j], p_r.at[j], neighbour)
        sent.append(copy)
        chunks[j]["p"] = copy

    eye = lax.broadcasted_iota(jnp.int32, (128, 128), 0) == lax.broadcasted_iota(
        jnp.int32, (128, 128), 1
    )
    row_scale = []
    for i in range(QUARTER // 128):
        line = cs_ref[:, pl.ds(pl.multiple_of(row * QUARTER + i * 128, 128), 128)]
        row_scale.append(jnp.sum(jnp.where(eye, line, 0.0), axis=1, keepdims=True))
    row_scale = jnp.concatenate(row_scale, axis=0)

    def finish(j):
        start, width = CHUNKS[j]
        cols = pl.ds(start, width)
        chunks[j]["c1"].wait_recv()
        chunks[j]["p"].wait_recv()
        total = c_keep[1, :, cols] + c_got[1, :, cols] + p_got[:, cols].astype(F32)
        col_scale = cs_ref[:, pl.ds(pl.multiple_of(col * WIDE + start, 128), width)]
        out_v[:, cols] = row_scale * total * col_scale
        copy = pltpu.make_async_copy(out_v.at[:, cols], out_ref.at[:, cols], o_s.at[j])
        copy.start()
        return copy

    outs = []
    send_b(0)
    send_a(0)
    send_b(1)
    send_a(1)
    send_b(2)
    wait_b(0)
    b_first(0)
    b_first(1)
    t1 = a_first(0)
    wait_b(1)
    b_second(0)
    b_first(2)
    t2 = a_second(0, t1)
    b_second(1)
    b_first(3)
    t3 = a_third(0, t1)
    u1 = a_first(1)
    b_third(0)
    t4 = a_fourth(0, t2)
    wait_b(2)
    b_second(2)
    b_third(1)
    b_first(4)
    u2 = a_second(1, u1)
    b_last(0)
    a_last(t3 + t4)
    multiply(0, 0)
    b_second(3)
    b_third(2)
    b_first(5)
    give(0)
    u3 = a_third(1, u1)
    b_last(1)
    multiply(1, 0)
    give(1)
    b_second(4)
    b_third(3)
    u4 = a_fourth(1, u2)
    b_last(2)
    multiply(2, 0)
    give(2)
    b_second(5)
    b_third(4)
    b_last(3)
    multiply(3, 0)
    give(3)
    a_last(u3 + u4)
    multiply(0, 1)
    multiply(1, 1)
    b_third(5)
    b_last(4)
    multiply(4, 0)
    give(4)
    multiply(2, 1)
    outs.append(finish(0))
    outs.append(finish(1))
    b_last(5)
    multiply(5, 0)
    give(5)
    multiply(3, 1)
    multiply(4, 1)
    multiply(5, 1)
    outs += [finish(j) for j in range(2, 6)]

    for copy in outs:
        copy.wait()
    for copy in sent:
        copy.wait_send()
    for h in range(2):
        ref = a_in.at[h, pl.ds(0, 7 * PAIRS_HERE), :]
        pltpu.make_async_copy(ref, ref, a2a_s.at[h]).wait()
    for g, (start, width) in enumerate(GROUPS):
        ref = bp.at[pl.ds(0, 7), 0, :, pl.ds(start, width)]
        pltpu.make_async_copy(ref, ref, a2a_s.at[2 + g]).wait()


def per_device(
    pair_valence, pair_conduction, elements, valence_energy, conduction_energy, coulomb_sqrt
):
    n = len(CHUNKS)
    smem = pl.BlockSpec(memory_space=pltpu.SMEM)
    vmem = pl.BlockSpec(memory_space=pltpu.VMEM)
    dma = pltpu.SemaphoreType.DMA
    return pl.pallas_call(
        kernel,
        out_shape=jax.ShapeDtypeStruct((QUARTER, WIDE), F32),
        in_specs=[smem, smem, vmem, vmem, vmem, vmem],
        out_specs=pl.BlockSpec(memory_space=pl.ANY),
        scratch_shapes=[
            pltpu.VMEM(elements.shape, BF16),
            pltpu.VMEM((2, 128, HALF), BF16),
            pltpu.VMEM((2, 8, HALF, 128), BF16),
            pltpu.VMEM((8, 8, PAIRS_HERE, WIDE), BF16),
            pltpu.VMEM((2, QUARTER, WIDE), F32),
            pltpu.VMEM((2, QUARTER, WIDE), F32),
            pltpu.VMEM((2, QUARTER, WIDE), F32),
            pltpu.VMEM((QUARTER, WIDE), BF16),
            pltpu.VMEM((QUARTER, WIDE), BF16),
            pltpu.VMEM((QUARTER, WIDE), F32),
            dma((5,)), dma((5,)),
            dma((2, 9)), dma((2, 9)),
            dma((n, 8)), dma((n, 8)),
            dma((n, 2)), dma((n, 2)),
            dma((n,)), dma((n,)),
            dma((n,)),
        ],
        compiler_params=pltpu.CompilerParams(
            collective_id=0, has_side_effects=True, vmem_limit_bytes=48 * 2**20
        ),
        cost_estimate=pl.CostEstimate(
            flops=2 * 1024 * WIDE * WIDE, bytes_accessed=3 * 2**20, transcendentals=0
        ),
    )(
        pair_valence,
        pair_conduction,
        elements,
        valence_energy.reshape(1, -1),
        conduction_energy.reshape(-1, 128),
        coulomb_sqrt.reshape(1, -1),
    )


def solution(mesh):
    placed = (P(("row", "col")), P(("row", "col")), P(("row", "col"), None), P(), P(), P())
    return jax.shard_map(
        per_device, mesh=mesh, in_specs=placed, out_specs=P("row", "col"), check_vma=False
    )
```

```python
import jax
import jax.numpy as jnp
from jax import lax
from jax.experimental import pallas as pl
from jax.experimental.pallas import tpu as pltpu
from jax.sharding import PartitionSpec as P

MESH = pl.DeviceIdType.MESH
F32, BF16 = jnp.float32, jnp.bfloat16

PAIRS_HERE = 16
WIDE = 1536
HALF = WIDE // 2
QUARTER = WIDE // 4
CHUNK = 256
CHUNKS = WIDE // CHUNK
GROUP = 2


def kernel(
    val_hbm, cond_hbm, e_hbm, ve_hbm, ce_hbm, cs_hbm, out_ref,
    val_ref, cond_ref, e_ref, ve_ref, ce_ref, cs_ref, in_s,
    es, a_in, at, bp, xs, c_own, c_got, p_give, p_got,
    a2a_s, a2a_r, ag_s, ag_r, bg_s, bg_r, c_s, c_r, p_s, p_r,
):
    loads = [
        pltpu.make_async_copy(far, near, in_s.at[i])
        for i, (far, near) in enumerate(
            (
                (e_hbm, e_ref), (val_hbm, val_ref), (cond_hbm, cond_ref),
                (ve_hbm, ve_ref), (ce_hbm, ce_ref), (cs_hbm, cs_ref),
            )
        )
    ]
    for load in loads:
        load.start()

    row, col = lax.axis_index("row"), lax.axis_index("col")
    core, x, zh = row % 2, (row // 2) % 4, row // 8
    y, zl = col // 2, col % 2
    xh, xl, z = x // 2, x % 2, zh * 2 + zl
    toward = 1 - 2 * zl

    def device(x_, y_, z_, core_):
        return ((z_ // 2 * 4 + x_) * 2 + core_, y_ * 2 + z_ % 2)

    def z_at(step):
        return (z + step + 8) % 8

    mirror = 3 - x
    mirror_dev = device(mirror, y, z, core)
    other_core = device(x, y, z, 1 - core)
    neighbour = device(x + 1 - 2 * xl, y, z, core)
    z_mate = device(x, y, z_at(toward), core)
    z1_up, z1_down = device(x, y, z_at(1), core), device(x, y, z_at(-1), core)
    z2_up, z2_down = device(x, y, z_at(2), core), device(x, y, z_at(-2), core)
    y_others = [(y + d) % 4 for d in (1, 3, 2)]
    y_up, y_down = device(x, y_others[0], z, core), device(x, y_others[1], z, core)
    near = [0, -toward, 2 * toward, -3 * toward]

    everyone = [z1_up, z1_down, z2_up, z2_down, device(x, y, z_at(-3 * toward), core)]
    everyone += [device(mirror, y, z_at(step), core) for step in near + [-2 * toward]]
    everyone += [device(x, y_, z, core) for y_ in y_others]
    everyone += [other_core, neighbour]
    barrier = pltpu.get_barrier_semaphore()
    for peer in everyone:
        pl.semaphore_signal(barrier, inc=1, device_id=peer, device_id_type=MESH)

    sent = []

    def send(src, dst, send_sem, recv_sem, peer):
        copy = pltpu.make_async_remote_copy(
            src_ref=src, dst_ref=dst, send_sem=send_sem, recv_sem=recv_sem,
            device_id=peer, device_id_type=MESH,
        )
        copy.start()
        return copy

    def wait_bytes(ref, sem):
        pltpu.make_async_copy(ref, ref, sem).wait()

    for load in loads:
        load.wait()

    def pick(idx_ref, table):
        slots = lax.broadcasted_iota(jnp.int32, table.shape, 0) * table.shape[1]
        slots += lax.broadcasted_iota(jnp.int32, table.shape, 1)
        rows = [
            jnp.sum(jnp.where(slots == idx_ref[i], table, 0.0), axis=0, keepdims=True)
            for i in range(PAIRS_HERE)
        ]
        return jnp.sum(jnp.concatenate(rows, axis=0), axis=1, keepdims=True)

    weight = 4.0 / (pick(val_ref, ve_ref[...]) - pick(cond_ref, ce_ref[...]))
    for j in range(0, e_ref.shape[1], HALF):
        part = e_ref[:, j : j + HALF].astype(F32)
        es[:, j : j + HALF] = (weight * part).astype(BF16)

    pl.semaphore_wait(barrier, len(everyone))

    own = zl + 3

    def send_b(g):
        for j in range(g * GROUP, g * GROUP + GROUP):

            def cols(y_, zl_):
                start = (y_ * 2 + zl_) * WIDE + j * CHUNK
                return pl.ds(pl.multiple_of(start, CHUNK), CHUNK)

            for y_ in y_others:
                for zl_, dst in ((zl, bp.at[j, own, xh, y]), (1 - zl, xs.at[j, y])):
                    send(
                        e_ref.at[:, cols(y_, zl_)], dst, a2a_s.at[2 + g], a2a_r.at[2 + g],
                        device(x, y_, z, core),
                    )
            bp[j, own, xh, y] = e_ref[:, cols(y, zl)]
            xs[j, y] = e_ref[:, cols(y, 1 - zl)]

    def wait_b(g):
        wait_bytes(bp.at[0, pl.ds(0, 3 * GROUP), 0, pl.ds(0, 2)], a2a_r.at[2 + g])

    def send_a(h):
        for step in near:
            z_ = z_at(step)
            place = (z - z_ // 2 * 2 + 11) % 8
            deep = pl.ds(place % 4 * 2 + xh, 1)
            for x_ in (x, mirror):
                part = 1 - x_ % 2 if h == 0 else x_ % 2
                start = (z_ // 2 * 2 + x_ // 2) * WIDE + part * HALF
                cols = pl.ds(pl.multiple_of(start, CHUNK), HALF)
                if x_ is x and step is near[0]:
                    a_in[h, place % 4 * 2 + xh] = es[:, cols]
                else:
                    send(
                        es.at[:, cols], a_in.at[h, place % 4 * 2 + xh],
                        a2a_s.at[h], a2a_r.at[h], device(x_, y, z_, core),
                    )

    def wait_a(h):
        wait_bytes(a_in.at[h, pl.ds(0, 7)], a2a_r.at[h])

    mate = y * 2 + 1 - zl
    up2, down2 = y_others[0] * 2, y_others[1] * 2

    def ag(h, n, slot, peer, rows=None):
        ref = at.at[h, slot] if rows is None else at.at[h, slot, pl.ds(*rows)]
        copy = send(ref, ref, ag_s.at[h, n], ag_r.at[h, n], peer)
        sent.append(copy)
        return copy

    def a_first(h):
        wait_a(h)
        at[h, col] = a_in[h].reshape(8 * PAIRS_HERE, HALF).T
        return [ag(h, 0, col, z_mate), ag(h, 1, col, y_up), ag(h, 2, col, y_down)]

    def a_second(h, first):
        first[0].wait_recv()
        return [ag(h, 3, mate, y_up), ag(h, 4, mate, y_down)]

    lo, hi = (0, QUARTER), (QUARTER, QUARTER)

    def a_third(h, first):
        first[1].wait_recv()
        one = ag(h, 5, down2 + zl, y_up, lo)
        first[2].wait_recv()
        return [one, ag(h, 6, up2 + zl, y_down, hi)]

    def a_fourth(h, second):
        second[0].wait_recv()
        one = ag(h, 7, down2 + 1 - zl, y_up, lo)
        second[1].wait_recv()
        return [one, ag(h, 8, up2 + 1 - zl, y_down, hi)]

    def a_last(copies):
        for copy in copies:
            copy.wait_recv()

    def bg(j, n, here, there, peer, rows=None):
        src, dst = (xs.at[j] if here is None else bp.at[j, here, xh]), bp.at[j, there, xh]
        if rows is not None:
            src, dst = src.at[pl.ds(*rows)], dst.at[pl.ds(*rows)]
        return send(src, dst, bg_s.at[j], bg_r.at[j, n], peer)

    def place_up(place, steps):
        return (place - 2 * steps + 8) % 8

    from_2d, from_2u, from_1d, from_1u, from_4, from_3d, from_3u = (
        (own + step + 8) % 8 for step in (-2, 2, -1, 1, 4, -3, 3)
    )

    chunks = [dict() for _ in range(CHUNKS)]

    def b_z(j):
        d = chunks[j]
        d["1u"] = bg(j, 0, None, place_up(own, zl), z1_up)
        d["1d"] = bg(j, 1, None, place_up(own, zl - 1), z1_down)
        d["2u"] = bg(j, 2, own, place_up(own, 1), z2_up)
        d["2d"] = bg(j, 3, own, place_up(own, -1), z2_down)

    def b_x(j, place=own):
        chunks[j]["m"] = bg(j, 8, place, place, mirror_dev)

    def b_second(j):
        d = chunks[j]
        d["1u"].wait_recv()
        d["3u"] = bg(j, 4, from_1d, place_up(from_1d, 1), z2_up)
        b_x(j, from_1d)
        d["1d"].wait_recv()
        d["3d"] = bg(j, 5, from_1u, place_up(from_1u, -1), z2_down)
        b_x(j, from_1u)
        d["2u"].wait_recv()
        d["4u"] = bg(j, 6, from_2d, place_up(from_2d, 1), z2_up, (0, 2))
        b_x(j, from_2d)
        d["2d"].wait_recv()
        d["4d"] = bg(j, 7, from_2u, place_up(from_2u, -1), z2_down, (2, 2))
        b_x(j, from_2u)

    def b_third(j):
        d = chunks[j]
        d["3u"].wait_recv()
        b_x(j, from_3d)
        d["3d"].wait_recv()
        b_x(j, from_3u)
        d["4u"].wait_recv()
        d["4d"].wait_recv()
        b_x(j, from_4)

    def b_last(j):
        wait_bytes(bp.at[j, :, 0], bg_r.at[j, 8])

    mine = pl.ds(pl.multiple_of(core * QUARTER, QUARTER), QUARTER)
    others = pl.ds(pl.multiple_of((1 - core) * QUARTER, QUARTER), QUARTER)

    def multiply(j, h):
        left = jnp.concatenate([at[h, n] for n in range(8)], axis=1)
        right = [
            bp[j, n % 2 * 4 : n % 2 * 4 + 4, :, n // 2].reshape(128, CHUNK) for n in range(8)
        ]
        right = jnp.concatenate(right, axis=0)
        c_own[j, h] = jnp.dot(left, right, preferred_element_type=F32)
        copy = send(c_own.at[j, h, others], c_got.at[j, h], c_s.at[j, h], c_r.at[j, h], other_core)
        sent.append(copy)
        chunks[j][f"c{h}"] = copy

    def give(j):
        chunks[j]["c0"].wait_recv()
        p_give[j] = (c_own[j, 0, mine] + c_got[j, 0]).astype(BF16)
        copy = send(p_give.at[j], p_got.at[j], p_s.at[j], p_r.at[j], neighbour)
        sent.append(copy)
        chunks[j]["p"] = copy

    eye = lax.broadcasted_iota(jnp.int32, (128, 128), 0) == lax.broadcasted_iota(
        jnp.int32, (128, 128), 1
    )
    row_scale = []
    for i in range(QUARTER // 128):
        line = cs_ref[:, pl.ds(pl.multiple_of(row * QUARTER + i * 128, 128), 128)]
        row_scale.append(jnp.sum(jnp.where(eye, line, 0.0), axis=1, keepdims=True))
    row_scale = jnp.concatenate(row_scale, axis=0)

    def finish(j):
        chunks[j]["c1"].wait_recv()
        chunks[j]["p"].wait_recv()
        total = c_own[j, 1, mine] + c_got[j, 1] + p_got[j].astype(F32)
        start = pl.multiple_of(col * WIDE + j * CHUNK, CHUNK)
        col_scale = cs_ref[:, pl.ds(start, CHUNK)]
        out_ref[:, j * CHUNK : (j + 1) * CHUNK] = row_scale * total * col_scale

    outs = []
    send_b(0)
    send_a(0)
    send_b(1)
    send_b(2)
    wait_b(0)
    b_z(0)
    b_x(0)
    b_x(1)
    b_z(1)
    wait_b(1)
    b_x(2)
    b_x(3)
    t1 = a_first(0)
    wait_b(2)
    b_x(4)
    b_x(5)
    b_second(0)
    b_second(1)
    b_z(2)
    t2 = a_second(0, t1)
    t3 = a_third(0, t1)
    b_z(3)
    b_third(0)
    b_third(1)
    send_a(1)
    t4 = a_fourth(0, t2)
    b_second(2)
    b_z(4)
    b_second(3)
    a_last(t3 + t4)
    b_last(0)
    multiply(0, 0)
    b_z(5)
    u1 = a_first(1)
    give(0)
    b_third(2)
    b_last(1)
    multiply(1, 0)
    b_third(3)
    give(1)
    b_second(4)
    u2 = a_second(1, u1)
    u3 = a_third(1, u1)
    b_second(5)
    b_last(2)
    multiply(2, 0)
    b_third(4)
    give(2)
    b_last(3)
    multiply(3, 0)
    b_third(5)
    u4 = a_fourth(1, u2)
    give(3)
    a_last(u3 + u4)
    multiply(0, 1)
    b_last(4)
    multiply(4, 0)
    multiply(1, 1)
    give(4)
    finish(0)
    multiply(2, 1)
    finish(1)
    b_last(5)
    multiply(5, 0)
    multiply(3, 1)
    give(5)
    finish(2)
    multiply(4, 1)
    finish(3)
    multiply(5, 1)
    finish(4)
    finish(5)

    for copy in outs:
        copy.wait()
    for copy in sent:
        copy.wait_send()
    for h in range(2):
        wait_bytes(a_in.at[h, pl.ds(0, 7)], a2a_s.at[h])
    for g in range(CHUNKS // GROUP):
        wait_bytes(bp.at[0, pl.ds(0, 3 * GROUP), 0, pl.ds(0, 2)], a2a_s.at[2 + g])
    for j in range(CHUNKS):
        wait_bytes(bp.at[pl.ds(0, 5), pl.ds(0, 3), 0], bg_s.at[j])


def per_device(
    pair_valence, pair_conduction, elements, valence_energy, conduction_energy, coulomb_sqrt
):
    n = CHUNKS
    dma = pltpu.SemaphoreType.DMA
    tables = (
        valence_energy.reshape(1, -1),
        conduction_energy.reshape(-1, 128),
        coulomb_sqrt.reshape(1, -1),
    )
    operands = [
        pltpu.with_memory_space_constraint(a, pltpu.HBM)
        for a in (pair_valence, pair_conduction, elements, *tables)
    ]
    return pl.pallas_call(
        kernel,
        out_shape=pltpu.VMEM((QUARTER, WIDE), F32),
        in_specs=[pl.BlockSpec(memory_space=pltpu.HBM)] * 6,
        out_specs=pl.BlockSpec(memory_space=pltpu.VMEM),
        scratch_shapes=[
            pltpu.SMEM((PAIRS_HERE,), jnp.int32),
            pltpu.SMEM((PAIRS_HERE,), jnp.int32),
            pltpu.VMEM(elements.shape, BF16),
            *(pltpu.VMEM(t.shape, F32) for t in tables),
            dma((6,)),
            pltpu.VMEM(elements.shape, BF16),
            pltpu.VMEM((2, 8, PAIRS_HERE, HALF), BF16),
            pltpu.VMEM((2, 8, HALF, 128), BF16),
            pltpu.VMEM((n, 8, 2, 4, PAIRS_HERE, CHUNK), BF16),
            pltpu.VMEM((n, 4, PAIRS_HERE, CHUNK), BF16),
            pltpu.VMEM((n, 2, HALF, CHUNK), F32),
            pltpu.VMEM((n, 2, QUARTER, CHUNK), F32),
            pltpu.VMEM((n, QUARTER, CHUNK), BF16),
            pltpu.VMEM((n, QUARTER, CHUNK), BF16),
            dma((5,)), dma((5,)),
            dma((2, 9)), dma((2, 9)),
            dma((n,)), dma((n, 9)),
            dma((n, 2)), dma((n, 2)),
            dma((n,)), dma((n,)),
        ],
        compiler_params=pltpu.CompilerParams(
            collective_id=0, has_side_effects=True, vmem_limit_bytes=48 * 2**20
        ),
        cost_estimate=pl.CostEstimate(
            flops=2 * 1024 * WIDE * WIDE, bytes_accessed=3 * 2**20, transcendentals=0
        ),
    )(*operands)


def solution(mesh):
    placed = (P(("row", "col")), P(("row", "col")), P(("row", "col"), None), P(), P(), P())
    return jax.shard_map(
        per_device, mesh=mesh, in_specs=placed, out_specs=P("row", "col"), check_vma=False
    )
```

```python
import jax
import jax.numpy as jnp
from jax import lax
from jax.experimental import pallas as pl
from jax.experimental.pallas import tpu as pltpu
from jax.sharding import PartitionSpec as P

MESH = pl.DeviceIdType.MESH
F32, BF16 = jnp.float32, jnp.bfloat16

PAIRS_HERE = 16
WIDE = 1536
HALF = WIDE // 2
QUARTER = WIDE // 4
CHUNKS = ((0, 256), (256, 256), (512, 256), (768, 256), (1024, 256), (1280, 128), (1408, 128))
GROUPS = ((0, 1), (2, 3), (4, 5, 6))
GROUP_WIDE = 512


def kernel(
    val_hbm, cond_hbm, e_hbm, ve_hbm, ce_hbm, cs_hbm, out_ref,
    val_ref, cond_ref, e_ref, ve_ref, ce_ref, cs_ref, in_s,
    es, a_in, at, bp, xs, c_give, c_got, p_give, p_got, d_own, d_got,
    a2a_s, a2a_r, ag_s, ag_r, bg_s, bg_r, c_s, c_r, d_s, d_r, p_s, p_r,
):
    loads = [
        pltpu.make_async_copy(far, near, in_s.at[i])
        for i, (far, near) in enumerate(
            (
                (e_hbm, e_ref), (val_hbm, val_ref), (cond_hbm, cond_ref),
                (ve_hbm, ve_ref), (ce_hbm, ce_ref), (cs_hbm, cs_ref),
            )
        )
    ]
    for load in loads:
        load.start()

    row, col = lax.axis_index("row"), lax.axis_index("col")
    core, x, zh = row % 2, (row // 2) % 4, row // 8
    y, zl = col // 2, col % 2
    xh, xl, z = x // 2, x % 2, zh * 2 + zl
    toward = 1 - 2 * zl

    def device(x_, y_, z_, core_):
        return ((z_ // 2 * 4 + x_) * 2 + core_, y_ * 2 + z_ % 2)

    def z_at(step):
        return (z + step + 8) % 8

    mirror = 3 - x
    mirror_dev = device(mirror, y, z, core)
    other_core = device(x, y, z, 1 - core)
    neighbour = device(x + 1 - 2 * xl, y, z, core)
    z_mate = device(x, y, z_at(toward), core)
    z1_up, z1_down = device(x, y, z_at(1), core), device(x, y, z_at(-1), core)
    z2_up, z2_down = device(x, y, z_at(2), core), device(x, y, z_at(-2), core)
    y_others = [(y + d) % 4 for d in (1, 3, 2)]
    y_up, y_down = device(x, y_others[0], z, core), device(x, y_others[1], z, core)
    near = [0, -toward, 2 * toward, -3 * toward]

    everyone = [z1_up, z1_down, z2_up, z2_down, device(x, y, z_at(-3 * toward), core)]
    everyone += [device(mirror, y, z_at(step), core) for step in near + [-2 * toward]]
    everyone += [device(x, y_, z, core) for y_ in y_others]
    everyone += [other_core, neighbour]
    barrier = pltpu.get_barrier_semaphore()
    for peer in everyone:
        pl.semaphore_signal(barrier, inc=1, device_id=peer, device_id_type=MESH)

    sent = []

    def send(src, dst, send_sem, recv_sem, peer):
        copy = pltpu.make_async_remote_copy(
            src_ref=src, dst_ref=dst, send_sem=send_sem, recv_sem=recv_sem,
            device_id=peer, device_id_type=MESH,
        )
        copy.start()
        return copy

    def wait_bytes(ref, sem):
        pltpu.make_async_copy(ref, ref, sem).wait()

    loads[0].wait()
    pl.semaphore_wait(barrier, len(everyone))

    own = zl + 3

    def send_b(g):
        for j in GROUPS[g]:
            first, wide = CHUNKS[j]

            def cols(y_, zl_):
                start = (y_ * 2 + zl_) * WIDE + first
                return pl.ds(pl.multiple_of(start, 128), wide)

            for y_ in y_others:
                for zl_, dst in ((zl, bp[j].at[own, xh, y]), (1 - zl, xs[j].at[y])):
                    send(
                        e_ref.at[:, cols(y_, zl_)], dst, a2a_s.at[2 + g], a2a_r.at[2 + g],
                        device(x, y_, z, core),
                    )
            bp[j][own, xh, y] = e_ref[:, cols(y, zl)]
            xs[j][y] = e_ref[:, cols(y, 1 - zl)]

    def wait_group(sem):
        wait_bytes(es.at[:, pl.ds(0, 3 * 2 * GROUP_WIDE)], sem)

    def wait_b(g):
        wait_group(a2a_r.at[2 + g])

    for g in range(len(GROUPS)):
        send_b(g)

    for load in loads[1:]:
        load.wait()

    def pick(idx_ref, table):
        slots = lax.broadcasted_iota(jnp.int32, table.shape, 0) * table.shape[1]
        slots += lax.broadcasted_iota(jnp.int32, table.shape, 1)
        rows = [
            jnp.sum(jnp.where(slots == idx_ref[i], table, 0.0), axis=0, keepdims=True)
            for i in range(PAIRS_HERE)
        ]
        return jnp.sum(jnp.concatenate(rows, axis=0), axis=1, keepdims=True)

    weight = 4.0 / (pick(val_ref, ve_ref[...]) - pick(cond_ref, ce_ref[...]))
    for j in range(0, e_ref.shape[1], HALF):
        part = e_ref[:, j : j + HALF].astype(F32)
        es[:, j : j + HALF] = (weight * part).astype(BF16)

    def send_a(h):
        for step in near[::-1]:
            z_ = z_at(step)
            place = (z - z_ // 2 * 2 + 11) % 8
            deep = pl.ds(place % 4 * 2 + xh, 1)
            for x_ in (mirror, x):
                part = 1 - x_ % 2 if h == 0 else x_ % 2
                start = (z_ // 2 * 2 + x_ // 2) * WIDE + part * HALF
                cols = pl.ds(pl.multiple_of(start, HALF), HALF)
                if x_ is x and step is near[0]:
                    a_in[h, place % 4 * 2 + xh] = es[:, cols]
                else:
                    send(
                        es.at[:, cols], a_in.at[h, place % 4 * 2 + xh],
                        a2a_s.at[h], a2a_r.at[h], device(x_, y, z_, core),
                    )

    def wait_a(h):
        wait_bytes(a_in.at[h, pl.ds(0, 7)], a2a_r.at[h])

    mate = y * 2 + 1 - zl
    up2, down2 = y_others[0] * 2, y_others[1] * 2

    def ag(h, n, slot, peer, rows=None):
        ref = at.at[h, slot] if rows is None else at.at[h, slot, pl.ds(*rows)]
        copy = send(ref, ref, ag_s.at[h, n], ag_r.at[h, n], peer)
        sent.append(copy)
        return copy

    halves = [dict(), dict()]
    lo, hi = (0, QUARTER), (QUARTER, QUARTER)

    def a_first(h):
        wait_a(h)
        at[h, col] = a_in[h].reshape(8 * PAIRS_HERE, HALF).T
        halves[h].update(
            mate_lo=ag(h, 0, col, z_mate, lo), mate_hi=ag(h, 1, col, z_mate, hi),
            up=ag(h, 2, col, y_up), down=ag(h, 3, col, y_down),
        )

    def a_third(h):
        d = halves[h]
        d["up"].wait_recv()
        d["far0"] = ag(h, 4, down2 + zl, y_up, lo)
        d["down"].wait_recv()
        d["far1"] = ag(h, 5, up2 + zl, y_down, hi)

    def a_second_lo(h):
        d = halves[h]
        d["mate_lo"].wait_recv()
        d.update(lo_up=ag(h, 6, mate, y_up, lo), lo_down=ag(h, 7, mate, y_down, lo))

    def a_second_hi(h):
        d = halves[h]
        d["mate_hi"].wait_recv()
        d.update(hi_up=ag(h, 8, mate, y_up, hi), hi_down=ag(h, 9, mate, y_down, hi))

    def a_fourth_lo(h):
        halves[h]["lo_up"].wait_recv()
        halves[h]["far2"] = ag(h, 10, down2 + 1 - zl, y_up, lo)

    def a_fourth_hi(h):
        halves[h]["hi_down"].wait_recv()
        halves[h]["far3"] = ag(h, 11, up2 + 1 - zl, y_down, hi)

    def a_last(h):
        for name in ("lo_down", "hi_up", "far0", "far1", "far2", "far3"):
            halves[h][name].wait_recv()

    def place_at(source, reader):
        there = z_at(reader * toward) // 2
        return (z + source * toward - 2 * there + 19) % 8

    def bg(j, n, source, step, rows=None):
        src = xs[j] if step in (1, -1) else bp[j].at[place_at(source, 0), xh]
        dst = bp[j].at[place_at(source, step), xh]
        if rows is not None:
            src, dst = src.at[pl.ds(*rows)], dst.at[pl.ds(*rows)]
        peer = device(x, y, z_at(step * toward), core)
        return send(src, dst, bg_s.at[j], bg_r.at[j, n], peer)

    chunks = [dict() for _ in CHUNKS]

    def b_z(j):
        chunks[j]["1t"] = bg(j, 0, 0, 1)
        chunks[j]["1a"] = bg(j, 1, 0, -1)
        chunks[j]["2t"] = bg(j, 2, 0, 2)
        chunks[j]["2a"] = bg(j, 3, 0, -2)

    def b_x(j, source=0):
        block = bp[j].at[place_at(source, 0), xh]
        send(block, block, bg_s.at[j], bg_r.at[j, 8], mirror_dev)

    def b_1t(j):
        chunks[j]["1t"].wait_recv()
        chunks[j]["3a"] = bg(j, 4, 1, -2)
        b_x(j, 1)

    def b_1a(j):
        chunks[j]["1a"].wait_recv()
        chunks[j]["3t"] = bg(j, 5, -1, 2)
        b_x(j, -1)

    def b_2t(j):
        chunks[j]["2t"].wait_recv()
        chunks[j]["4t"] = bg(j, 6, -2, 2, (0, 2))
        b_x(j, -2)

    def b_2a(j):
        chunks[j]["2a"].wait_recv()
        chunks[j]["4a"] = bg(j, 7, 2, -2, (2, 2))
        b_x(j, 2)

    def b_3t(j):
        chunks[j]["3t"].wait_recv()
        b_x(j, -3)

    def b_3a(j):
        chunks[j]["3a"].wait_recv()
        b_x(j, 3)

    def b_4(j):
        chunks[j]["4t"].wait_recv()
        chunks[j]["4a"].wait_recv()
        b_x(j, 4)

    def b_last(j):
        wait_bytes(bp[j].at[:, 0], bg_r.at[j, 8])

    def rows_of(q):
        return pl.ds(pl.multiple_of(q * QUARTER, QUARTER), QUARTER)

    def columns(j):
        wide = CHUNKS[j][1]
        parts = [bp[j][n % 2 * 4 : n % 2 * 4 + 4, :, n // 2].reshape(128, wide) for n in range(8)]
        return jnp.concatenate(parts, axis=0)

    def product(h, right, out, got, send_sem, recv_sem):
        @pl.loop(0, 2)
        def _(i):
            rows = rows_of((1 - core + i) % 2)
            left = jnp.concatenate([at[h, n, rows] for n in range(8)], axis=1)
            out[rows] = jnp.dot(left, right, preferred_element_type=F32)

            @pl.when(i == 0)
            def _():
                send(out.at[rows], got, send_sem, recv_sem, other_core)

    def multiply(j):
        product(0, columns(j), c_give[j], c_got[j], c_s.at[j], c_r.at[j])

    def multiply_own(g):
        right = jnp.concatenate([columns(j) for j in GROUPS[g]], axis=1)
        product(1, right, d_own.at[g], d_got.at[g], d_s.at[g], d_r.at[g])

    def give(j):
        wait_bytes(c_got[j], c_r.at[j])
        p_give[j][...] = (c_give[j][rows_of(core)] + c_got[j][...]).astype(BF16)
        sent.append(send(p_give[j], p_got[j], p_s.at[j], p_r.at[j], neighbour))

    eye = lax.broadcasted_iota(jnp.int32, (128, 128), 0) == lax.broadcasted_iota(
        jnp.int32, (128, 128), 1
    )
    row_scale = []
    for i in range(QUARTER // 128):
        line = cs_ref[:, pl.ds(pl.multiple_of(row * QUARTER + i * 128, 128), 128)]
        row_scale.append(jnp.sum(jnp.where(eye, line, 0.0), axis=1, keepdims=True))
    row_scale = jnp.concatenate(row_scale, axis=0)

    def finish_own(g):
        wait_bytes(d_got.at[g], d_r.at[g])
        d_got[g] += d_own[g, rows_of(core)]

    def finish(j):
        wait_bytes(p_got[j], p_r.at[j])
        first, wide = CHUNKS[j]
        in_group = pl.ds(first % GROUP_WIDE, wide)
        total = d_got[first // GROUP_WIDE, :, in_group] + p_got[j][...].astype(F32)
        start = pl.multiple_of(col * WIDE + first, 128)
        col_scale = cs_ref[:, pl.ds(start, wide)]
        out_ref[:, first : first + wide] = row_scale * total * col_scale

    outs = []
    send_a(0)
    wait_b(0)
    b_z(0)
    b_x(0)
    b_x(1)
    b_z(1)
    wait_b(1)
    b_x(2)
    b_x(3)
    a_first(0)
    wait_b(2)
    b_x(4)
    b_x(5)
    b_x(6)
    b_1t(0)
    b_1a(0)
    b_2t(0)
    b_2a(0)
    b_1t(1)
    b_1a(1)
    b_2t(1)
    b_2a(1)
    b_z(2)
    a_third(0)
    a_second_lo(0)
    b_z(3)
    a_second_hi(0)
    send_a(1)
    b_3t(0)
    b_3a(0)
    b_4(0)
    b_3t(1)
    b_3a(1)
    b_4(1)
    a_fourth_lo(0)
    b_1t(2)
    b_1a(2)
    b_2t(2)
    b_2a(2)
    b_z(4)
    a_fourth_hi(0)
    b_1t(3)
    b_1a(3)
    b_2t(3)
    b_2a(3)
    b_z(5)
    b_z(6)
    a_last(0)
    b_last(0)
    multiply(0)
    a_first(1)
    b_3t(2)
    b_3a(2)
    b_4(2)
    give(0)
    b_last(1)
    multiply(1)
    b_3t(3)
    b_3a(3)
    b_4(3)
    b_1t(4)
    b_1a(4)
    b_2t(4)
    b_2a(4)
    give(1)
    b_last(2)
    multiply(2)
    a_third(1)
    a_second_lo(1)
    b_1t(5)
    b_1a(5)
    b_2t(5)
    b_2a(5)
    a_second_hi(1)
    give(2)
    b_1t(6)
    b_1a(6)
    b_2t(6)
    b_2a(6)
    b_3t(4)
    b_3a(4)
    b_4(4)
    b_last(3)
    multiply(3)
    b_3t(5)
    b_3a(5)
    b_4(5)
    a_fourth_lo(1)
    b_3t(6)
    b_3a(6)
    b_4(6)
    give(3)
    a_fourth_hi(1)
    b_last(4)
    multiply(4)
    b_last(5)
    give(4)
    multiply(5)
    b_last(6)
    multiply(6)
    give(5)
    a_last(1)
    give(6)
    multiply_own(0)
    multiply_own(1)
    multiply_own(2)
    finish_own(0)
    finish(0)
    finish(1)
    finish_own(1)
    finish(2)
    finish(3)
    finish_own(2)
    finish(4)
    finish(5)
    finish(6)

    for copy in outs:
        copy.wait()
    for copy in sent:
        copy.wait_send()
    for h in range(2):
        wait_bytes(a_in.at[h, pl.ds(0, 7)], a2a_s.at[h])
    for g in range(len(GROUPS)):
        wait_group(a2a_s.at[2 + g])
        wait_bytes(d_got.at[g], d_s.at[g])
    for j, (_, wide) in enumerate(CHUNKS):
        wait_bytes(c_got[j], c_s.at[j])
        wait_bytes(at.at[0, pl.ds(0, 5), pl.ds(0, 12 * wide // 8)], bg_s.at[j])


def per_device(
    pair_valence, pair_conduction, elements, valence_energy, conduction_energy, coulomb_sqrt
):
    n = len(CHUNKS)

    def each(*shape, dtype=BF16):
        return [pltpu.VMEM((*shape, wide), dtype) for _, wide in CHUNKS]

    dma = pltpu.SemaphoreType.DMA
    tables = (
        valence_energy.reshape(1, -1),
        conduction_energy.reshape(-1, 128),
        coulomb_sqrt.reshape(1, -1),
    )
    operands = [
        pltpu.with_memory_space_constraint(a, pltpu.HBM)
        for a in (pair_valence, pair_conduction, elements, *tables)
    ]
    return pl.pallas_call(
        kernel,
        out_shape=pltpu.VMEM((QUARTER, WIDE), F32),
        in_specs=[pl.BlockSpec(memory_space=pltpu.HBM)] * 6,
        out_specs=pl.BlockSpec(memory_space=pltpu.VMEM),
        scratch_shapes=[
            pltpu.SMEM((PAIRS_HERE,), jnp.int32),
            pltpu.SMEM((PAIRS_HERE,), jnp.int32),
            pltpu.VMEM(elements.shape, BF16),
            *(pltpu.VMEM(t.shape, F32) for t in tables),
            dma((6,)),
            pltpu.VMEM(elements.shape, BF16),
            pltpu.VMEM((2, 8, PAIRS_HERE, HALF), BF16),
            pltpu.VMEM((2, 8, HALF, 128), BF16),
            each(8, 2, 4, PAIRS_HERE),
            each(4, PAIRS_HERE),
            each(HALF, dtype=F32),
            each(QUARTER, dtype=F32),
            each(QUARTER),
            each(QUARTER),
            pltpu.VMEM((len(GROUPS), HALF, GROUP_WIDE), F32),
            pltpu.VMEM((len(GROUPS), QUARTER, GROUP_WIDE), F32),
            dma((5,)), dma((5,)),
            dma((2, 12)), dma((2, 12)),
            dma((n,)), dma((n, 9)),
            dma((n,)), dma((n,)),
            dma((len(GROUPS),)), dma((len(GROUPS),)),
            dma((n,)), dma((n,)),
        ],
        compiler_params=pltpu.CompilerParams(
            collective_id=0, has_side_effects=True, vmem_limit_bytes=48 * 2**20
        ),
        cost_estimate=pl.CostEstimate(
            flops=2 * 1024 * WIDE * WIDE, bytes_accessed=3 * 2**20, transcendentals=0
        ),
    )(*operands)


def solution(mesh):
    placed = (P(("row", "col")), P(("row", "col")), P(("row", "col"), None), P(), P(), P())
    return jax.shard_map(
        per_device, mesh=mesh, in_specs=placed, out_specs=P("row", "col"), check_vma=False
    )
```

```python
import jax
import jax.numpy as jnp
from jax import lax
from jax.experimental import pallas as pl
from jax.experimental.pallas import tpu as pltpu
from jax.sharding import PartitionSpec as P

MESH = pl.DeviceIdType.MESH
F32, BF16 = jnp.float32, jnp.bfloat16

PAIRS_HERE = 16
WIDE = 1536
HALF = WIDE // 2
QUARTER = WIDE // 4
CHUNKS = ((0, 256), (256, 256), (512, 256), (768, 256), (1024, 128), (1152, 128), (1280, 128), (1408, 128))
GROUPS = ((0, 1), (2, 3), (4, 5, 6, 7))
GROUP_WIDE = 512


def kernel(
    val_hbm, cond_hbm, e_hbm, ve_hbm, ce_hbm, cs_hbm, out_ref,
    val_ref, cond_ref, e_ref, ve_ref, ce_ref, cs_ref, in_s,
    es, a_in, at, bp, xs, c_give, c_got, p_give, p_got, d_own, d_got,
    a2a_s, a2a_r, ag_s, ag_r, bg_s, bg_r, c_s, c_r, d_r, p_s, p_r,
):
    loads = [
        pltpu.make_async_copy(far, near, in_s.at[i])
        for i, (far, near) in enumerate(
            (
                (e_hbm, e_ref), (val_hbm, val_ref), (cond_hbm, cond_ref),
                (ve_hbm, ve_ref), (ce_hbm, ce_ref), (cs_hbm, cs_ref),
            )
        )
    ]
    for load in loads:
        load.start()

    row, col = lax.axis_index("row"), lax.axis_index("col")
    core, x, zh = row % 2, (row // 2) % 4, row // 8
    y, zl = col // 2, col % 2
    xh, xl, z = x // 2, x % 2, zh * 2 + zl
    toward = 1 - 2 * zl

    def device(x_, y_, z_, core_):
        return ((z_ // 2 * 4 + x_) * 2 + core_, y_ * 2 + z_ % 2)

    def z_at(step):
        return (z + step + 8) % 8

    mirror = 3 - x
    mirror_dev = device(mirror, y, z, core)
    other_core = device(x, y, z, 1 - core)
    neighbour = device(x + 1 - 2 * xl, y, z, core)
    z_mate = device(x, y, z_at(toward), core)
    z1_up, z1_down = device(x, y, z_at(1), core), device(x, y, z_at(-1), core)
    z2_up, z2_down = device(x, y, z_at(2), core), device(x, y, z_at(-2), core)
    y_others = [(y + d) % 4 for d in (1, 3, 2)]
    y_up, y_down = device(x, y_others[0], z, core), device(x, y_others[1], z, core)
    near = [0, -toward, 2 * toward, -3 * toward]

    everyone = [z1_up, z1_down, z2_up, z2_down, device(x, y, z_at(-3 * toward), core)]
    everyone += [device(mirror, y, z_at(step), core) for step in near + [-2 * toward]]
    everyone += [device(x, y_, z, core) for y_ in y_others]
    everyone += [other_core, neighbour]
    barrier = pltpu.get_barrier_semaphore()
    for peer in everyone:
        pl.semaphore_signal(barrier, inc=1, device_id=peer, device_id_type=MESH)

    def send(src, dst, send_sem, recv_sem, peer):
        copy = pltpu.make_async_remote_copy(
            src_ref=src, dst_ref=dst, send_sem=send_sem, recv_sem=recv_sem,
            device_id=peer, device_id_type=MESH,
        )
        copy.start()
        return copy

    def wait_bytes(ref, sem):
        pltpu.make_async_copy(ref, ref, sem).wait()

    loads[0].wait()
    pl.semaphore_wait(barrier, len(everyone))

    own = zl + 3

    def send_b(g):
        for j in GROUPS[g]:
            first, wide = CHUNKS[j]

            def cols(y_, zl_):
                start = (y_ * 2 + zl_) * WIDE + first
                return pl.ds(pl.multiple_of(start, 128), wide)

            for y_ in y_others:
                for zl_, dst in ((zl, bp[j].at[own, xh, y]), (1 - zl, xs[j].at[y])):
                    send(
                        e_ref.at[:, cols(y_, zl_)], dst, a2a_s, a2a_r.at[2 + g],
                        device(x, y_, z, core),
                    )
            bp[j][own, xh, y] = e_ref[:, cols(y, zl)]
            xs[j][y] = e_ref[:, cols(y, 1 - zl)]

    def wait_group(sem):
        wait_bytes(es.at[:, pl.ds(0, 3 * 2 * GROUP_WIDE)], sem)

    def wait_b(g):
        wait_group(a2a_r.at[2 + g])

    for g in range(len(GROUPS)):
        send_b(g)

    for load in loads[1:]:
        load.wait()

    def pick(idx_ref, table):
        slots = lax.broadcasted_iota(jnp.int32, table.shape, 0) * table.shape[1]
        slots += lax.broadcasted_iota(jnp.int32, table.shape, 1)
        rows = [
            jnp.sum(jnp.where(slots == idx_ref[i], table, 0.0), axis=0, keepdims=True)
            for i in range(PAIRS_HERE)
        ]
        return jnp.sum(jnp.concatenate(rows, axis=0), axis=1, keepdims=True)

    weight = 4.0 / (pick(val_ref, ve_ref[...]) - pick(cond_ref, ce_ref[...]))
    for j in range(0, e_ref.shape[1], HALF):
        part = e_ref[:, j : j + HALF].astype(F32)
        es[:, j : j + HALF] = (weight * part).astype(BF16)

    def send_a(h):
        for step in near[::-1]:
            z_ = z_at(step)
            place = (z - z_ // 2 * 2 + 11) % 8
            deep = pl.ds(place % 4 * 2 + xh, 1)
            for x_ in (mirror, x):
                part = 1 - x_ % 2 if h == 0 else x_ % 2
                start = (z_ // 2 * 2 + x_ // 2) * WIDE + part * HALF
                cols = pl.ds(pl.multiple_of(start, HALF), HALF)
                if x_ is x and step is near[0]:
                    a_in[h, place % 4 * 2 + xh] = es[:, cols]
                else:
                    send(
                        es.at[:, cols], a_in.at[h, place % 4 * 2 + xh],
                        a2a_s, a2a_r.at[h], device(x_, y, z_, core),
                    )

    def wait_a(h):
        wait_bytes(a_in.at[h, pl.ds(0, 7)], a2a_r.at[h])

    mate = y * 2 + 1 - zl
    up2, down2 = y_others[0] * 2, y_others[1] * 2

    def ag(h, n, slot, peer, rows=None):
        ref = at.at[h, slot] if rows is None else at.at[h, slot, pl.ds(*rows)]
        return send(ref, ref, ag_s, ag_r.at[h, n], peer)

    halves = [dict(), dict()]
    lo, hi = (0, QUARTER), (QUARTER, QUARTER)

    def a_first(h):
        wait_a(h)
        at[h, col] = a_in[h].reshape(8 * PAIRS_HERE, HALF).T
        halves[h].update(
            mate_lo=ag(h, 0, col, z_mate, lo), mate_hi=ag(h, 1, col, z_mate, hi),
        )
        ag(h, 2, col, y_up)
        ag(h, 2, col, y_down)

    def a_third(h):
        wait_bytes(at.at[h, pl.ds(0, 2)], ag_r.at[h, 2])
        ag(h, 3, down2 + zl, y_up, lo)
        ag(h, 3, up2 + zl, y_down, hi)

    def a_second_lo(h):
        d = halves[h]
        d["mate_lo"].wait_recv()
        d["lo_up"] = ag(h, 4, mate, y_up, lo)
        ag(h, 3, mate, y_down, lo)

    def a_second_hi(h):
        d = halves[h]
        d["mate_hi"].wait_recv()
        ag(h, 3, mate, y_up, hi)
        d["hi_down"] = ag(h, 5, mate, y_down, hi)

    def a_fourth_lo(h):
        halves[h]["lo_up"].wait_recv()
        ag(h, 3, down2 + 1 - zl, y_up, lo)

    def a_fourth_hi(h):
        halves[h]["hi_down"].wait_recv()
        ag(h, 3, up2 + 1 - zl, y_down, hi)

    def a_last(h):
        wait_bytes(at.at[h, pl.ds(0, 3)], ag_r.at[h, 3])

    def place_at(source, reader):
        there = z_at(reader * toward) // 2
        return (z + source * toward - 2 * there + 19) % 8

    def bg(j, n, source, step, rows=None):
        src = xs[j] if step in (1, -1) else bp[j].at[place_at(source, 0), xh]
        dst = bp[j].at[place_at(source, step), xh]
        if rows is not None:
            src, dst = src.at[pl.ds(*rows)], dst.at[pl.ds(*rows)]
        peer = device(x, y, z_at(step * toward), core)
        return send(src, dst, bg_s, bg_r.at[j, n], peer)

    def b_z(j):
        bg(j, 0, 0, 1)
        bg(j, 0, 0, -1)
        bg(j, 1, 0, 2)
        bg(j, 1, 0, -2)

    def b_x(j, source=0):
        block = bp[j].at[place_at(source, 0), xh]
        send(block, block, bg_s, bg_r.at[j, 3], mirror_dev)

    def b_1(j):
        wait_bytes(bp[j].at[pl.ds(0, 2), 0], bg_r.at[j, 0])
        bg(j, 2, 1, -2)
        b_x(j, 1)
        bg(j, 2, -1, 2)
        b_x(j, -1)

    def b_2(j):
        wait_bytes(bp[j].at[pl.ds(0, 2), 0], bg_r.at[j, 1])
        bg(j, 2, -2, 2, (0, 2))
        b_x(j, -2)
        bg(j, 2, 2, -2, (2, 2))
        b_x(j, 2)

    def b_3(j):
        wait_bytes(bp[j].at[pl.ds(0, 3), 0], bg_r.at[j, 2])
        b_x(j, -3)
        b_x(j, 3)
        b_x(j, 4)

    def b_last(j):
        wait_bytes(bp[j].at[:, 0], bg_r.at[j, 3])

    def rows_of(q):
        return pl.ds(pl.multiple_of(q * QUARTER, QUARTER), QUARTER)

    def columns(j):
        wide = CHUNKS[j][1]
        parts = [bp[j][n % 2 * 4 : n % 2 * 4 + 4, :, n // 2].reshape(128, wide) for n in range(8)]
        return jnp.concatenate(parts, axis=0)

    def product(h, right, out, got, send_sem, recv_sem):
        @pl.loop(0, 2)
        def _(i):
            rows = rows_of((1 - core + i) % 2)
            left = jnp.concatenate([at[h, n, rows] for n in range(8)], axis=1)
            out[rows] = jnp.dot(left, right, preferred_element_type=F32)

            @pl.when(i == 0)
            def _():
                send(out.at[rows], got, send_sem, recv_sem, other_core)

    def multiply(j):
        product(0, columns(j), c_give[j], c_got[j], c_s, c_r.at[j])

    def multiply_own(g):
        right = jnp.concatenate([columns(j) for j in GROUPS[g]], axis=1)
        product(1, right, d_own.at[g], d_got.at[g], c_s, d_r.at[g])

    def give(j):
        wait_bytes(c_got[j], c_r.at[j])
        p_give[j][...] = (c_give[j][rows_of(core)] + c_got[j][...]).astype(BF16)
        send(p_give[j], p_got[j], p_s, p_r.at[j], neighbour)

    eye = lax.broadcasted_iota(jnp.int32, (128, 128), 0) == lax.broadcasted_iota(
        jnp.int32, (128, 128), 1
    )
    row_scale = []
    for i in range(QUARTER // 128):
        line = cs_ref[:, pl.ds(pl.multiple_of(row * QUARTER + i * 128, 128), 128)]
        row_scale.append(jnp.sum(jnp.where(eye, line, 0.0), axis=1, keepdims=True))
    row_scale = jnp.concatenate(row_scale, axis=0)

    def finish_own(g):
        wait_bytes(d_got.at[g], d_r.at[g])
        d_got[g] += d_own[g, rows_of(core)]

    def finish(j):
        wait_bytes(p_got[j], p_r.at[j])
        first, wide = CHUNKS[j]
        in_group = pl.ds(first % GROUP_WIDE, wide)
        total = d_got[first // GROUP_WIDE, :, in_group] + p_got[j][...].astype(F32)
        start = pl.multiple_of(col * WIDE + first, 128)
        col_scale = cs_ref[:, pl.ds(start, wide)]
        out_ref[:, first : first + wide] = row_scale * total * col_scale

    outs = []
    send_a(0)
    wait_b(0)
    b_z(0)
    b_x(0)
    b_x(1)
    b_z(1)
    wait_b(1)
    b_x(2)
    b_x(3)
    a_first(0)
    wait_b(2)
    b_x(4)
    b_x(5)
    b_x(6)
    b_x(7)
    b_1(0)
    b_2(0)
    b_1(1)
    b_2(1)
    b_z(2)
    a_third(0)
    a_second_lo(0)
    b_z(3)
    a_second_hi(0)
    send_a(1)
    b_3(0)
    b_3(1)
    a_fourth_lo(0)
    b_1(2)
    b_2(2)
    b_z(4)
    a_fourth_hi(0)
    b_1(3)
    b_2(3)
    b_z(5)
    b_z(6)
    b_z(7)
    a_last(0)
    b_last(0)
    multiply(0)
    a_first(1)
    b_3(2)
    give(0)
    b_last(1)
    multiply(1)
    b_3(3)
    b_1(4)
    b_2(4)
    give(1)
    b_last(2)
    multiply(2)
    a_third(1)
    a_second_lo(1)
    b_1(5)
    b_2(5)
    a_second_hi(1)
    give(2)
    b_1(6)
    b_1(7)
    b_2(6)
    b_2(7)
    b_3(4)
    b_last(3)
    multiply(3)
    b_3(5)
    a_fourth_lo(1)
    b_3(6)
    b_3(7)
    give(3)
    a_fourth_hi(1)
    b_last(4)
    multiply(4)
    b_last(5)
    give(4)
    multiply(5)
    b_last(6)
    b_last(7)
    multiply(6)
    multiply(7)
    give(5)
    a_last(1)
    give(6)
    give(7)
    multiply_own(0)
    multiply_own(1)
    multiply_own(2)
    finish_own(0)
    finish(0)
    finish(1)
    finish_own(1)
    finish(2)
    finish(3)
    finish_own(2)
    finish(4)
    finish(5)
    finish(6)
    finish(7)

    for copy in outs:
        copy.wait()
    wait_bytes(at.at[0, pl.ds(0, 4), pl.ds(0, 624)], a2a_s)
    wait_bytes(at.at[:, pl.ds(0, 7)], ag_s)
    wait_bytes(at.at[:, :, pl.ds(0, 720)], bg_s)
    wait_bytes(d_own, c_s)
    wait_bytes(at.at[0, pl.ds(0, 6)], p_s)


def per_device(
    pair_valence, pair_conduction, elements, valence_energy, conduction_energy, coulomb_sqrt
):
    n = len(CHUNKS)

    def each(*shape, dtype=BF16):
        return [pltpu.VMEM((*shape, wide), dtype) for _, wide in CHUNKS]

    dma = pltpu.SemaphoreType.DMA
    tables = (
        valence_energy.reshape(1, -1),
        conduction_energy.reshape(-1, 128),
        coulomb_sqrt.reshape(1, -1),
    )
    operands = [
        pltpu.with_memory_space_constraint(a, pltpu.HBM)
        for a in (pair_valence, pair_conduction, elements, *tables)
    ]
    return pl.pallas_call(
        kernel,
        out_shape=pltpu.VMEM((QUARTER, WIDE), F32),
        in_specs=[pl.BlockSpec(memory_space=pltpu.HBM)] * 6,
        out_specs=pl.BlockSpec(memory_space=pltpu.VMEM),
        scratch_shapes=[
            pltpu.SMEM((PAIRS_HERE,), jnp.int32),
            pltpu.SMEM((PAIRS_HERE,), jnp.int32),
            pltpu.VMEM(elements.shape, BF16),
            *(pltpu.VMEM(t.shape, F32) for t in tables),
            dma((6,)),
            pltpu.VMEM(elements.shape, BF16),
            pltpu.VMEM((2, 8, PAIRS_HERE, HALF), BF16),
            pltpu.VMEM((2, 8, HALF, 128), BF16),
            each(8, 2, 4, PAIRS_HERE),
            each(4, PAIRS_HERE),
            each(HALF, dtype=F32),
            each(QUARTER, dtype=F32),
            each(QUARTER),
            each(QUARTER),
            pltpu.VMEM((len(GROUPS), HALF, GROUP_WIDE), F32),
            pltpu.VMEM((len(GROUPS), QUARTER, GROUP_WIDE), F32),
            dma, dma((5,)),
            dma, dma((2, 6)),
            dma, dma((n, 4)),
            dma, dma((n,)),
            dma((len(GROUPS),)),
            dma, dma((n,)),
        ],
        compiler_params=pltpu.CompilerParams(
            collective_id=0, has_side_effects=True, vmem_limit_bytes=48 * 2**20
        ),
        cost_estimate=pl.CostEstimate(
            flops=2 * 1024 * WIDE * WIDE, bytes_accessed=3 * 2**20, transcendentals=0
        ),
    )(*operands)


def solution(mesh):
    placed = (P(("row", "col")), P(("row", "col")), P(("row", "col"), None), P(), P(), P())
    return jax.shard_map(
        per_device, mesh=mesh, in_specs=placed, out_specs=P("row", "col"), check_vma=False
    )
```

```python
import jax
import jax.numpy as jnp
from jax import lax
from jax.experimental import pallas as pl
from jax.experimental.pallas import tpu as pltpu
from jax.sharding import PartitionSpec as P

MESH = pl.DeviceIdType.MESH
F32, BF16 = jnp.float32, jnp.bfloat16

PAIRS_HERE = 16
WIDE = 1536
HALF = WIDE // 2
QUARTER = WIDE // 4
CHUNKS = ((0, 256), (256, 256), (512, 256), (768, 256), (1024, 128), (1152, 128), (1280, 128), (1408, 128))
GROUPS = ((0, 1), (2, 3), (4, 5, 6, 7))
GROUP_WIDE = 512


def kernel(
    val_hbm, cond_hbm, e_hbm, ve_hbm, ce_hbm, cs_hbm, out_ref,
    val_ref, cond_ref, e_ref, ve_ref, ce_ref, cs_ref, in_s,
    es, a_in, at, bp, xs, c_give, c_got, p_give, p_got, d_own, d_got,
    a2a_s, a2a_r, ag_s, ag_r, bg_s, bg_r, c_s, c_r, d_r, p_s, p_r,
):
    loads = [
        pltpu.make_async_copy(far, near, in_s.at[i])
        for i, (far, near) in enumerate(
            (
                (e_hbm, e_ref), (val_hbm, val_ref), (cond_hbm, cond_ref),
                (ve_hbm, ve_ref), (ce_hbm, ce_ref), (cs_hbm, cs_ref),
            )
        )
    ]
    for load in loads:
        load.start()

    row, col = lax.axis_index("row"), lax.axis_index("col")
    core, x, zh = row % 2, (row // 2) % 4, row // 8
    y, zl = col // 2, col % 2
    xh, xl, z = x // 2, x % 2, zh * 2 + zl
    toward = 1 - 2 * zl

    def device(x_, y_, z_, core_):
        return ((z_ // 2 * 4 + x_) * 2 + core_, y_ * 2 + z_ % 2)

    def z_at(step):
        return (z + step + 8) % 8

    mirror = 3 - x
    mirror_dev = device(mirror, y, z, core)
    other_core = device(x, y, z, 1 - core)
    neighbour = device(x + 1 - 2 * xl, y, z, core)
    z_mate = device(x, y, z_at(toward), core)
    z1_up, z1_down = device(x, y, z_at(1), core), device(x, y, z_at(-1), core)
    z2_up, z2_down = device(x, y, z_at(2), core), device(x, y, z_at(-2), core)
    y_others = [(y + d) % 4 for d in (1, 3, 2)]
    y_up, y_down = device(x, y_others[0], z, core), device(x, y_others[1], z, core)
    near = [0, -toward, 2 * toward, -3 * toward]

    everyone = [z1_up, z1_down, z2_up, z2_down, device(x, y, z_at(-3 * toward), core)]
    everyone += [device(mirror, y, z_at(step), core) for step in near + [-2 * toward]]
    everyone += [device(x, y_, z, core) for y_ in y_others]
    everyone += [other_core, neighbour]
    barrier = pltpu.get_barrier_semaphore()
    for peer in everyone:
        pl.semaphore_signal(barrier, inc=1, device_id=peer, device_id_type=MESH)

    def send(src, dst, send_sem, recv_sem, peer):
        copy = pltpu.make_async_remote_copy(
            src_ref=src, dst_ref=dst, send_sem=send_sem, recv_sem=recv_sem,
            device_id=peer, device_id_type=MESH,
        )
        copy.start()
        return copy

    def wait_bytes(ref, sem):
        pltpu.make_async_copy(ref, ref, sem).wait()

    loads[0].wait()
    for load in loads[1:]:
        load.wait()

    def pick(idx_ref, table):
        slots = lax.broadcasted_iota(jnp.int32, table.shape, 0) * table.shape[1]
        slots += lax.broadcasted_iota(jnp.int32, table.shape, 1)
        rows = [
            jnp.sum(jnp.where(slots == idx_ref[i], table, 0.0), axis=0, keepdims=True)
            for i in range(PAIRS_HERE)
        ]
        return jnp.sum(jnp.concatenate(rows, axis=0), axis=1, keepdims=True)

    weight = 4.0 / (pick(val_ref, ve_ref[...]) - pick(cond_ref, ce_ref[...]))
    for j in range(0, e_ref.shape[1], HALF):
        part = e_ref[:, j : j + HALF].astype(F32)
        es[:, j : j + HALF] = (weight * part).astype(BF16)

    pl.semaphore_wait(barrier, len(everyone))

    own = zl + 3

    def send_b(g):
        for j in GROUPS[g]:
            first, wide = CHUNKS[j]

            def cols(y_, zl_):
                start = (y_ * 2 + zl_) * WIDE + first
                return pl.ds(pl.multiple_of(start, 128), wide)

            for y_ in y_others:
                for zl_, dst in ((zl, bp[j].at[own, xh, y]), (1 - zl, xs[j].at[y])):
                    send(
                        e_ref.at[:, cols(y_, zl_)], dst, a2a_s, a2a_r.at[2 + g],
                        device(x, y_, z, core),
                    )
            bp[j][own, xh, y] = e_ref[:, cols(y, zl)]
            xs[j][y] = e_ref[:, cols(y, 1 - zl)]

    def wait_group(sem):
        wait_bytes(es.at[:, pl.ds(0, 3 * 2 * GROUP_WIDE)], sem)

    def wait_b(g):
        wait_group(a2a_r.at[2 + g])

    for g in range(len(GROUPS)):
        send_b(g)

    def send_a(h):
        for step in near[::-1]:
            z_ = z_at(step)
            place = (z - z_ // 2 * 2 + 11) % 8
            deep = pl.ds(place % 4 * 2 + xh, 1)
            for x_ in (mirror, x):
                part = 1 - x_ % 2 if h == 0 else x_ % 2
                start = (z_ // 2 * 2 + x_ // 2) * WIDE + part * HALF
                cols = pl.ds(pl.multiple_of(start, HALF), HALF)
                if x_ is x and step is near[0]:
                    a_in[h, place % 4 * 2 + xh] = es[:, cols]
                else:
                    send(
                        es.at[:, cols], a_in.at[h, place % 4 * 2 + xh],
                        a2a_s, a2a_r.at[h], device(x_, y, z_, core),
                    )

    def wait_a(h):
        wait_bytes(a_in.at[h, pl.ds(0, 7)], a2a_r.at[h])

    mate = y * 2 + 1 - zl
    up2, down2 = y_others[0] * 2, y_others[1] * 2

    def ag(h, n, slot, peer, rows=None):
        ref = at.at[h, slot] if rows is None else at.at[h, slot, pl.ds(*rows)]
        return send(ref, ref, ag_s, ag_r.at[h, n], peer)

    halves = [dict(), dict()]
    lo, hi = (0, QUARTER), (QUARTER, QUARTER)

    def a_first(h):
        wait_a(h)
        at[h, col] = a_in[h].reshape(8 * PAIRS_HERE, HALF).T
        halves[h].update(
            mate_lo=ag(h, 0, col, z_mate, lo), mate_hi=ag(h, 1, col, z_mate, hi),
        )
        ag(h, 2, col, y_up)
        ag(h, 2, col, y_down)

    def a_third(h):
        wait_bytes(at.at[h, pl.ds(0, 2)], ag_r.at[h, 2])
        ag(h, 3, down2 + zl, y_up, lo)
        ag(h, 3, up2 + zl, y_down, hi)

    def a_second_lo(h):
        d = halves[h]
        d["mate_lo"].wait_recv()
        d["lo_up"] = ag(h, 4, mate, y_up, lo)
        ag(h, 3, mate, y_down, lo)

    def a_second_hi(h):
        d = halves[h]
        d["mate_hi"].wait_recv()
        ag(h, 3, mate, y_up, hi)
        d["hi_down"] = ag(h, 5, mate, y_down, hi)

    def a_fourth_lo(h):
        halves[h]["lo_up"].wait_recv()
        ag(h, 3, down2 + 1 - zl, y_up, lo)

    def a_fourth_hi(h):
        halves[h]["hi_down"].wait_recv()
        ag(h, 3, up2 + 1 - zl, y_down, hi)

    def a_last(h):
        wait_bytes(at.at[h, pl.ds(0, 3)], ag_r.at[h, 3])

    def place_at(source, reader):
        there = z_at(reader * toward) // 2
        return (z + source * toward - 2 * there + 19) % 8

    def bg(j, n, source, step, rows=None):
        src = xs[j] if step in (1, -1) else bp[j].at[place_at(source, 0), xh]
        dst = bp[j].at[place_at(source, step), xh]
        if rows is not None:
            src, dst = src.at[pl.ds(*rows)], dst.at[pl.ds(*rows)]
        peer = device(x, y, z_at(step * toward), core)
        return send(src, dst, bg_s, bg_r.at[j, n], peer)

    def b_z(j):
        bg(j, 0, 0, 1)
        bg(j, 0, 0, -1)
        bg(j, 1, 0, 2)
        bg(j, 1, 0, -2)

    def b_x(j, source=0):
        block = bp[j].at[place_at(source, 0), xh]
        send(block, block, bg_s, bg_r.at[j, 3], mirror_dev)

    def b_1(j):
        wait_bytes(bp[j].at[pl.ds(0, 2), 0], bg_r.at[j, 0])
        bg(j, 2, 1, -2)
        b_x(j, 1)
        bg(j, 2, -1, 2)
        b_x(j, -1)

    def b_2(j):
        wait_bytes(bp[j].at[pl.ds(0, 2), 0], bg_r.at[j, 1])
        bg(j, 2, -2, 2, (0, 2))
        b_x(j, -2)
        bg(j, 2, 2, -2, (2, 2))
        b_x(j, 2)

    def b_3(j):
        wait_bytes(bp[j].at[pl.ds(0, 3), 0], bg_r.at[j, 2])
        b_x(j, -3)
        b_x(j, 3)
        b_x(j, 4)

    def b_last(j):
        wait_bytes(bp[j].at[:, 0], bg_r.at[j, 3])

    def rows_of(q):
        return pl.ds(pl.multiple_of(q * QUARTER, QUARTER), QUARTER)

    def columns(j):
        wide = CHUNKS[j][1]
        parts = [bp[j][n % 2 * 4 : n % 2 * 4 + 4, :, n // 2].reshape(128, wide) for n in range(8)]
        return jnp.concatenate(parts, axis=0)

    def product(h, right, out, got, send_sem, recv_sem):
        @pl.loop(0, 2)
        def _(i):
            rows = rows_of((1 - core + i) % 2)
            left = jnp.concatenate([at[h, n, rows] for n in range(8)], axis=1)
            out[rows] = jnp.dot(left, right, preferred_element_type=F32)

            @pl.when(i == 0)
            def _():
                send(out.at[rows], got, send_sem, recv_sem, other_core)

    def multiply(j):
        product(0, columns(j), c_give[j], c_got[j], c_s, c_r.at[j])

    def multiply_own(g):
        right = jnp.concatenate([columns(j) for j in GROUPS[g]], axis=1)
        product(1, right, d_own.at[g], d_got.at[g], c_s, d_r.at[g])

    def give(j):
        wait_bytes(c_got[j], c_r.at[j])
        p_give[j][...] = (c_give[j][rows_of(core)] + c_got[j][...]).astype(BF16)
        send(p_give[j], p_got[j], p_s, p_r.at[j], neighbour)

    eye = lax.broadcasted_iota(jnp.int32, (128, 128), 0) == lax.broadcasted_iota(
        jnp.int32, (128, 128), 1
    )
    row_scale = []
    for i in range(QUARTER // 128):
        line = cs_ref[:, pl.ds(pl.multiple_of(row * QUARTER + i * 128, 128), 128)]
        row_scale.append(jnp.sum(jnp.where(eye, line, 0.0), axis=1, keepdims=True))
    row_scale = jnp.concatenate(row_scale, axis=0)

    def finish_own(g):
        wait_bytes(d_got.at[g], d_r.at[g])
        d_got[g] += d_own[g, rows_of(core)]

    def finish(j):
        wait_bytes(p_got[j], p_r.at[j])
        first, wide = CHUNKS[j]
        in_group = pl.ds(first % GROUP_WIDE, wide)
        total = d_got[first // GROUP_WIDE, :, in_group] + p_got[j][...].astype(F32)
        start = pl.multiple_of(col * WIDE + first, 128)
        col_scale = cs_ref[:, pl.ds(start, wide)]
        out_ref[:, first : first + wide] = row_scale * total * col_scale

    outs = []
    send_a(0)
    wait_b(0)
    b_z(0)
    b_x(0)
    b_x(1)
    b_z(1)
    wait_b(1)
    b_x(2)
    b_x(3)
    a_first(0)
    wait_b(2)
    b_x(4)
    b_x(5)
    b_x(6)
    b_x(7)
    b_1(0)
    b_2(0)
    b_1(1)
    b_2(1)
    b_z(2)
    a_third(0)
    a_second_lo(0)
    b_z(3)
    a_second_hi(0)
    send_a(1)
    b_3(0)
    b_3(1)
    a_fourth_lo(0)
    b_1(2)
    b_2(2)
    b_z(4)
    a_fourth_hi(0)
    b_1(3)
    b_2(3)
    b_z(5)
    b_z(6)
    b_z(7)
    a_last(0)
    b_last(0)
    multiply(0)
    a_first(1)
    b_3(2)
    give(0)
    b_last(1)
    multiply(1)
    b_3(3)
    b_1(4)
    b_2(4)
    give(1)
    b_last(2)
    multiply(2)
    a_third(1)
    a_second_lo(1)
    b_1(5)
    b_2(5)
    a_second_hi(1)
    give(2)
    b_1(6)
    b_1(7)
    b_2(6)
    b_2(7)
    b_3(4)
    b_last(3)
    multiply(3)
    b_3(5)
    a_fourth_lo(1)
    b_3(6)
    b_3(7)
    give(3)
    a_fourth_hi(1)
    b_last(4)
    multiply(4)
    b_last(5)
    give(4)
    multiply(5)
    b_last(6)
    b_last(7)
    multiply(6)
    multiply(7)
    give(5)
    a_last(1)
    give(6)
    give(7)
    multiply_own(0)
    multiply_own(1)
    multiply_own(2)
    finish_own(0)
    finish(0)
    finish(1)
    finish_own(1)
    finish(2)
    finish(3)
    finish_own(2)
    finish(4)
    finish(5)
    finish(6)
    finish(7)

    for copy in outs:
        copy.wait()
    wait_bytes(at.at[0, pl.ds(0, 4), pl.ds(0, 624)], a2a_s)
    wait_bytes(at.at[:, pl.ds(0, 7)], ag_s)
    wait_bytes(at.at[:, :, pl.ds(0, 720)], bg_s)
    wait_bytes(d_own, c_s)
    wait_bytes(at.at[0, pl.ds(0, 6)], p_s)


def per_device(
    pair_valence, pair_conduction, elements, valence_energy, conduction_energy, coulomb_sqrt
):
    n = len(CHUNKS)

    def each(*shape, dtype=BF16):
        return [pltpu.VMEM((*shape, wide), dtype) for _, wide in CHUNKS]

    dma = pltpu.SemaphoreType.DMA
    tables = (
        valence_energy.reshape(1, -1),
        conduction_energy.reshape(-1, 128),
        coulomb_sqrt.reshape(1, -1),
    )
    operands = [
        pltpu.with_memory_space_constraint(a, pltpu.HBM)
        for a in (pair_valence, pair_conduction, elements, *tables)
    ]
    return pl.pallas_call(
        kernel,
        out_shape=pltpu.VMEM((QUARTER, WIDE), F32),
        in_specs=[pl.BlockSpec(memory_space=pltpu.HBM)] * 6,
        out_specs=pl.BlockSpec(memory_space=pltpu.VMEM),
        scratch_shapes=[
            pltpu.SMEM((PAIRS_HERE,), jnp.int32),
            pltpu.SMEM((PAIRS_HERE,), jnp.int32),
            pltpu.VMEM(elements.shape, BF16),
            *(pltpu.VMEM(t.shape, F32) for t in tables),
            dma((6,)),
            pltpu.VMEM(elements.shape, BF16),
            pltpu.VMEM((2, 8, PAIRS_HERE, HALF), BF16),
            pltpu.VMEM((2, 8, HALF, 128), BF16),
            each(8, 2, 4, PAIRS_HERE),
            each(4, PAIRS_HERE),
            each(HALF, dtype=F32),
            each(QUARTER, dtype=F32),
            each(QUARTER),
            each(QUARTER),
            pltpu.VMEM((len(GROUPS), HALF, GROUP_WIDE), F32),
            pltpu.VMEM((len(GROUPS), QUARTER, GROUP_WIDE), F32),
            dma, dma((5,)),
            dma, dma((2, 6)),
            dma, dma((n, 4)),
            dma, dma((n,)),
            dma((len(GROUPS),)),
            dma, dma((n,)),
        ],
        compiler_params=pltpu.CompilerParams(
            collective_id=0, has_side_effects=True, vmem_limit_bytes=48 * 2**20
        ),
        cost_estimate=pl.CostEstimate(
            flops=2 * 1024 * WIDE * WIDE, bytes_accessed=3 * 2**20, transcendentals=0
        ),
    )(*operands)


def solution(mesh):
    placed = (P(("row", "col")), P(("row", "col")), P(("row", "col"), None), P(), P(), P())
    return jax.shard_map(
        per_device, mesh=mesh, in_specs=placed, out_specs=P("row", "col"), check_vma=False
    )
```
